512 devices in a mesh: band: 32 (over z_hi, x, core), grid: 16 (over y, z_lo).
Axes of the slice: x: 4, y: 8, z: 8 (z_hi: 4, z_lo: 2; z = z_hi * 2 + z_lo), core: 2. Of those that a mesh axis runs over, the one named last changes fastest.
Arguments:
- orbitals: bfloat16 [32, 96, 9216], P('band', 'grid'), may hold values from -6 to 6
Outputs:
- exchanged: float32 [32, 96, 9216], P('band', 'grid')
The draws below stay inside these ranges and needn't reach their ends.
All inputs are finite; a program needn't handle non-finite values.
Results may differ from the reference program's by a relative error of at most 0.0003.
Values may be sent and summed in bfloat16 or wider, within the bound.
No kernel may reach another device: no remote copies, remote signals or barrier semaphores. Data moves between devices by JAX's collectives and lax.ppermute only.
A program may use at most 64 MiB of HBM per device.

```python
import math
import jax
import jax.numpy as jnp
from jax import lax

NG = 96
PLANE = 9216
BANDS = 32


def levels(own_key, dims, shards, low, high):
    gain, own = 1.0, jax.random.fold_in(own_key, 6)
    for axis_at, parts in shards:
        draws = jnp.exp(jax.random.uniform(jax.random.fold_in(own, axis_at), (parts,), jnp.float32, low / len(shards), high / len(shards)))
        gain = gain * jnp.repeat(draws, dims[axis_at] // parts).reshape([-1 if axis == axis_at else 1 for axis in range(len(dims))])
    return gain


def gaussian(own_key, dims, scale, most, split=(), held_as=jnp.bfloat16):
    array = jax.random.normal(own_key, dims, jnp.float32) * scale
    if len(split) > 0:
        array = levels(own_key, dims, split, -0.22, 0.18) * array
    return jnp.clip(array, min=-most, max=most).astype(held_as)


def setup_inputs(seed: int = 0) -> dict:
    key_list = jax.random.split(jax.random.key(seed), 2)
    orbitals = gaussian(key_list[0], (BANDS, NG, PLANE), 1.0, 6.0, ((0, 32), (1, 16)))
    return {"orbitals": orbitals}


MIXING = 0.25
SPACING = 0.31
SCREENING = 0.106


def kernel_values(index_x, index_y, index_z, length):
    def wavenumber(positions):
        signed = jnp.where(positions * 2 < length, positions, positions - length).astype(jnp.float32)
        return signed * (2.0 * math.pi / (length * SPACING))

    wave_x = wavenumber(index_x)[:, None, None]
    wave_y = wavenumber(index_y)[None, :, None]
    wave_z = wavenumber(index_z)[None, None, :]
    square = wave_x * wave_x + wave_y * wave_y + wave_z * wave_z
    safe_square = jnp.where(square > 0, square, 1.0)
    values = 4.0 * math.pi * (1.0 - jnp.exp(-safe_square / (4.0 * SCREENING * SCREENING))) / safe_square
    return jnp.where(square > 0, values, 0.0)


def reference(orbitals):
    orbital_cells = orbitals.astype(jnp.float32).reshape(BANDS, NG, NG, NG)
    span_index = jnp.arange(NG, dtype=jnp.int32)
    kernel_grid = kernel_values(span_index, span_index, span_index, NG)

    def one_band(unused_carry, band_cells):
        density = band_cells[None] * orbital_cells
        spectrum = jnp.fft.fftn(density, axes=(1, 2, 3))
        potential = jnp.real(jnp.fft.ifftn(kernel_grid[None] * spectrum, axes=(1, 2, 3)))
        return unused_carry, -MIXING * jnp.sum(potential * orbital_cells, axis=0)

    unused_carry, exchange_rows = lax.scan(one_band, jnp.zeros((), jnp.float32), orbital_cells)
    return exchange_rows.reshape(BANDS, NG, NG * NG)
```

```python
import math

import jax
import jax.numpy as jnp
import numpy as np
from jax import lax
from jax.experimental import pallas as pl
from jax.experimental.pallas import tpu as pltpu
from jax.sharding import Mesh
from jax.sharding import PartitionSpec as P

MIXING = 0.25
SPACING = 0.31
SCREENING = 0.106

NG = 96
LANES = 128
SLAB = 6
BF16 = jnp.bfloat16
F32 = jnp.float32
AXES = ("zh", "x", "core", "y", "zl")
SIZES = (4, 4, 2, 8, 2)
BAND = ("zh", "x", "core")
GRID = ("y", "zl")
X_BLOCK = 8
KY_BLOCK = 8


def cas_halves():
    index = np.arange(NG)
    phases = (index[:, None] * index[None, :] % NG) * (2.0 * math.pi / NG)
    table = np.cos(phases) + np.sin(phases)
    high = table.astype(BF16)
    low = (table - high.astype(np.float64)).astype(BF16)
    return high, low


def right_table():
    high, low = cas_halves()
    table = np.zeros((2 * LANES, 2 * LANES), BF16)
    for row in (0, LANES):
        table[row : row + NG, 0:NG] = high
        table[row : row + NG, LANES : LANES + NG] = low
    return table


def left_table():
    high, low = cas_halves()
    return np.concatenate(
        [np.concatenate([high, high], axis=1), np.concatenate([low, low], axis=1)], axis=0
    )


def kernel_table():
    index = jnp.arange(NG, dtype=jnp.int32)
    signed = jnp.where(index * 2 < NG, index, index - NG).astype(F32)
    wave = signed * (2.0 * math.pi / (NG * SPACING))
    wave_z = jnp.pad(wave, (0, LANES - NG))
    square = (
        (wave * wave)[:, None, None] + (wave * wave)[None, :, None] + (wave_z * wave_z)[None, None, :]
    )
    safe = jnp.where(square > 0, square, 1.0)
    values = 4.0 * math.pi * (1.0 - jnp.exp(-safe / (4.0 * SCREENING * SCREENING))) / safe
    return jnp.where(square > 0, values, 0.0) * (-MIXING / float(NG) ** 3)


def halves(values):
    high = values.astype(BF16)
    low = (values - high.astype(F32)).astype(BF16)
    return high, low


def left_transform(table, columns):
    high, low = halves(columns)
    both = jnp.dot(table, jnp.concatenate([high, low], axis=0), preferred_element_type=F32)
    return both[:NG] + both[NG:]


def right_transform(rows, table):
    high, low = halves(rows)
    both = jnp.dot(jnp.concatenate([high, low], axis=1), table, preferred_element_type=F32)
    return both[:, :LANES] + both[:, LANES:]


def padded(plane):
    return jnp.concatenate([plane, jnp.zeros((plane.shape[0], LANES - NG), plane.dtype)], axis=1)


def forward_kernel(own_ref, first_ref, second_ref, right_ref, left_ref, out_ref):
    for at in range(X_BLOCK):
        own = own_ref[at].astype(F32)
        first = own * first_ref[at].astype(F32)
        second = own * second_ref[at].astype(F32)
        rows = jnp.concatenate([padded(first), padded(second)], axis=0)
        rows = right_transform(rows, right_ref[...])
        columns = jnp.concatenate([rows[:NG], rows[NG:]], axis=1)
        out_ref[at] = left_transform(left_ref[...], columns)


def middle_kernel(field_ref, kernel_ref, left_ref, out_ref):
    for at in range(KY_BLOCK):
        columns = left_transform(left_ref[...], field_ref[:, at, :])
        weight = kernel_ref[at]
        columns = columns * jnp.concatenate([weight, weight], axis=1)
        out_ref[:, at, :] = left_transform(left_ref[...], columns)


def backward_kernel(field_ref, first_ref, second_ref, right_ref, left_ref, out_ref):
    for at in range(X_BLOCK):
        columns = left_transform(left_ref[...], field_ref[at])
        rows = jnp.concatenate([columns[:, :LANES], columns[:, LANES:]], axis=0)
        rows = right_transform(rows, right_ref[...])
        first = rows[:NG, :NG] * first_ref[at].astype(F32)
        second = rows[NG:, :NG] * second_ref[at].astype(F32)
        out_ref[at] = first + second


PARAMS = pltpu.CompilerParams(vmem_limit_bytes=48 * 1024 * 1024)
CUBE = (NG, NG, NG)
WIDE = (NG, NG, 2 * LANES)
RIGHT_SPEC = pl.BlockSpec((2 * LANES, 2 * LANES), lambda i: (0, 0))
LEFT_SPEC = pl.BlockSpec((2 * NG, 2 * NG), lambda i: (0, 0))


def forward(own, first, second, right, left):
    orbital = pl.BlockSpec((X_BLOCK, NG, NG), lambda i: (i, 0, 0))
    return pl.pallas_call(
        forward_kernel,
        grid=(NG // X_BLOCK,),
        in_specs=[orbital, orbital, orbital, RIGHT_SPEC, LEFT_SPEC],
        out_specs=pl.BlockSpec((X_BLOCK, NG, 2 * LANES), lambda i: (i, 0, 0)),
        out_shape=jax.ShapeDtypeStruct(WIDE, F32),
        compiler_params=PARAMS,
    )(own, first, second, right, left)


def middle(field, kernel, left):
    block = pl.BlockSpec((NG, KY_BLOCK, 2 * LANES), lambda i: (0, i, 0))
    return pl.pallas_call(
        middle_kernel,
        grid=(NG // KY_BLOCK,),
        in_specs=[block, pl.BlockSpec((KY_BLOCK, NG, LANES), lambda i: (i, 0, 0)), LEFT_SPEC],
        out_specs=block,
        out_shape=jax.ShapeDtypeStruct(WIDE, F32),
        compiler_params=PARAMS,
    )(field, kernel, left)


def backward(field, first, second, right, left):
    orbital = pl.BlockSpec((X_BLOCK, NG, NG), lambda i: (i, 0, 0))
    return pl.pallas_call(
        backward_kernel,
        grid=(NG // X_BLOCK,),
        in_specs=[
            pl.BlockSpec((X_BLOCK, NG, 2 * LANES), lambda i: (i, 0, 0)),
            orbital,
            orbital,
            RIGHT_SPEC,
            LEFT_SPEC,
        ],
        out_specs=orbital,
        out_shape=jax.ShapeDtypeStruct(CUBE, F32),
        compiler_params=PARAMS,
    )(field, first, second, right, left)


def exchanged_slabs(slab):
    pairs = []
    for pair in range(16):
        for core in range(2):
            for place in range(16):
                pairs.append(((pair * 2 + core) * 16 + place, (place * 2 + core) * 16 + pair))
    return lax.ppermute(slab, AXES, pairs)


def body(orbitals):
    slab = orbitals.reshape(SLAB * NG * NG // LANES, LANES)
    right = jnp.asarray(right_table())
    left = jnp.asarray(left_table())
    kernel = kernel_table()
    first = lax.all_gather(exchanged_slabs(slab), ("zh", "x"), axis=0, tiled=True).reshape(CUBE)
    second = lax.ppermute(first, "core", [(0, 1), (1, 0)])
    own = lax.all_gather(slab, GRID, axis=0, tiled=True).reshape(CUBE)
    field = forward(own, first, second, right, left)
    field = middle(field, kernel, left)
    terms = backward(field, first, second, right, left).reshape(NG * NG * NG // LANES, LANES)
    total = lax.psum_scatter(terms, GRID, scatter_dimension=0, tiled=True)
    return total.reshape(orbitals.shape)


def solution(mesh):
    fine = Mesh(mesh.devices.reshape(SIZES), AXES)
    placed = P(BAND, GRID, None)
    return jax.shard_map(
        body, mesh=fine, in_specs=(placed,), out_specs=placed, check_vma=False
    )
```

```python
import math

import jax
import jax.numpy as jnp
import numpy as np
from jax import lax
from jax.experimental import pallas as pl
from jax.experimental.pallas import tpu as pltpu
from jax.sharding import Mesh
from jax.sharding import PartitionSpec as P

MIXING = 0.25
SPACING = 0.31
SCREENING = 0.106

NG = 96
LANES = 128
SLAB = 6
BF16 = jnp.bfloat16
F32 = jnp.float32
AXES = ("zh", "x", "core", "y", "zl")
SIZES = (4, 4, 2, 8, 2)
BAND = ("zh", "x", "core")
GRID = ("y", "zl")
X_BLOCK = 8
KY_BLOCK = 8


def cas_halves():
    index = np.arange(NG)
    phases = (index[:, None] * index[None, :] % NG) * (2.0 * math.pi / NG)
    table = np.cos(phases) + np.sin(phases)
    high = table.astype(BF16)
    low = (table - high.astype(np.float64)).astype(BF16)
    return high, low


def right_table():
    high, low = cas_halves()
    table = np.zeros((2 * LANES, 2 * LANES), BF16)
    for row in (0, LANES):
        table[row : row + NG, 0:NG] = high
        table[row : row + NG, LANES : LANES + NG] = low
    return table


def left_table():
    high, low = cas_halves()
    return np.concatenate(
        [np.concatenate([high, high], axis=1), np.concatenate([low, low], axis=1)], axis=0
    )


def kernel_table():
    index = jnp.arange(NG, dtype=jnp.int32)
    signed = jnp.where(index * 2 < NG, index, index - NG).astype(F32)
    wave = signed * (2.0 * math.pi / (NG * SPACING))
    wave_z = jnp.pad(wave, (0, LANES - NG))
    square = (
        (wave * wave)[:, None, None] + (wave * wave)[None, :, None] + (wave_z * wave_z)[None, None, :]
    )
    safe = jnp.where(square > 0, square, 1.0)
    values = 4.0 * math.pi * (1.0 - jnp.exp(-safe / (4.0 * SCREENING * SCREENING))) / safe
    return jnp.where(square > 0, values, 0.0) * (-MIXING / float(NG) ** 3)


def halves(values):
    high = values.astype(BF16)
    low = (values - high.astype(F32)).astype(BF16)
    return high, low


def left_transform(table, columns):
    high, low = halves(columns)
    both = jnp.dot(table, jnp.concatenate([high, low], axis=0), preferred_element_type=F32)
    return both[:NG] + both[NG:]


def right_transform(rows, table):
    high, low = halves(rows)
    both = jnp.dot(jnp.concatenate([high, low], axis=1), table, preferred_element_type=F32)
    return both[:, :LANES] + both[:, LANES:]


PACKED = NG * NG // LANES
TAIL = NG - PACKED
REST = LANES - NG


def pack(planes):
    tail = planes[:, PACKED:]
    thirds = [tail[:, :, REST * at : REST * (at + 1)] for at in range(NG // REST)]
    return jnp.concatenate([planes[:, :PACKED], jnp.concatenate(thirds, axis=1)], axis=2)


def unpack(packed):
    side = packed[:, :, NG:]
    thirds = [side[:, TAIL * at : TAIL * (at + 1)] for at in range(NG // REST)]
    return jnp.concatenate([packed[:, :, :NG], jnp.concatenate(thirds, axis=2)], axis=1)


def lane_mask(rows, low, high):
    lane = lax.broadcasted_iota(jnp.int32, (rows, LANES), 1)
    return (lane >= low) & (lane < high)


def unpack_plane(packed):
    top = jnp.where(lane_mask(PACKED, 0, NG), packed, 0.0)
    tail = jnp.zeros((TAIL, LANES), packed.dtype)
    for at in range(NG // REST):
        rolled = pltpu.roll(packed[TAIL * at : TAIL * (at + 1)], REST * (at + 1), 1)
        tail = jnp.where(lane_mask(TAIL, REST * at, REST * (at + 1)), rolled, tail)
    return jnp.concatenate([top, tail], axis=0)


def pack_plane(plane):
    tail = plane[PACKED:]
    sides = [pltpu.roll(tail, LANES - REST * (at + 1), 1) for at in range(NG // REST)]
    return jnp.where(lane_mask(PACKED, 0, NG), plane[:PACKED], jnp.concatenate(sides, axis=0))


def forward_kernel(own_ref, first_ref, second_ref, right_ref, left_ref, out_ref):
    for at in range(X_BLOCK):
        own = own_ref[at].astype(F32)
        first = unpack_plane(own * first_ref[at].astype(F32))
        second = unpack_plane(own * second_ref[at].astype(F32))
        rows = right_transform(jnp.concatenate([first, second], axis=0), right_ref[...])
        columns = jnp.concatenate([rows[:NG], rows[NG:]], axis=1)
        columns = left_transform(left_ref[...], columns)
        out_ref[0, at] = columns[:, :LANES]
        out_ref[1, at] = columns[:, LANES:]


def middle_kernel(field_ref, kernel_ref, left_ref, out_ref):
    field = field_ref.reshape(2 * NG * KY_BLOCK, LANES)
    out = out_ref.reshape(2 * NG * KY_BLOCK, LANES)
    for at in range(KY_BLOCK):
        first = pl.ds(at, NG, stride=KY_BLOCK)
        second = pl.ds(NG * KY_BLOCK + at, NG, stride=KY_BLOCK)
        columns = jnp.concatenate([field[first, :], field[second, :]], axis=1)
        columns = left_transform(left_ref[...], columns)
        weight = kernel_ref[at]
        columns = columns * jnp.concatenate([weight, weight], axis=1)
        columns = left_transform(left_ref[...], columns)
        out[first, :] = columns[:, :LANES]
        out[second, :] = columns[:, LANES:]


def backward_kernel(field_ref, first_ref, second_ref, right_ref, left_ref, out_ref):
    for at in range(X_BLOCK):
        columns = jnp.concatenate([field_ref[0, at], field_ref[1, at]], axis=1)
        columns = left_transform(left_ref[...], columns)
        rows = jnp.concatenate([columns[:, :LANES], columns[:, LANES:]], axis=0)
        rows = right_transform(rows, right_ref[...])
        first = pack_plane(rows[:NG]) * first_ref[at].astype(F32)
        second = pack_plane(rows[NG:]) * second_ref[at].astype(F32)
        out_ref[at] = first + second


PARAMS = pltpu.CompilerParams(vmem_limit_bytes=48 * 1024 * 1024)
CUBE = (NG, PACKED, LANES)
WIDE = (2, NG, NG, LANES)
RIGHT_SPEC = pl.BlockSpec((2 * LANES, 2 * LANES), lambda i: (0, 0))
LEFT_SPEC = pl.BlockSpec((2 * NG, 2 * NG), lambda i: (0, 0))
ORBITAL_SPEC = pl.BlockSpec((X_BLOCK, PACKED, LANES), lambda i: (i, 0, 0))
FIELD_SPEC = pl.BlockSpec((2, X_BLOCK, NG, LANES), lambda i: (0, i, 0, 0))


def forward(own, first, second, right, left):
    return pl.pallas_call(
        forward_kernel,
        grid=(NG // X_BLOCK,),
        in_specs=[ORBITAL_SPEC, ORBITAL_SPEC, ORBITAL_SPEC, RIGHT_SPEC, LEFT_SPEC],
        out_specs=FIELD_SPEC,
        out_shape=jax.ShapeDtypeStruct(WIDE, F32),
        compiler_params=PARAMS,
        name="forward",
    )(own, first, second, right, left)


def middle(field, kernel, left):
    block = pl.BlockSpec((2, NG, KY_BLOCK, LANES), lambda i: (0, 0, i, 0))
    return pl.pallas_call(
        middle_kernel,
        grid=(NG // KY_BLOCK,),
        in_specs=[block, pl.BlockSpec((KY_BLOCK, NG, LANES), lambda i: (i, 0, 0)), LEFT_SPEC],
        out_specs=block,
        out_shape=jax.ShapeDtypeStruct(WIDE, F32),
        compiler_params=PARAMS,
        name="middle",
    )(field, kernel, left)


def backward(field, first, second, right, left):
    return pl.pallas_call(
        backward_kernel,
        grid=(NG // X_BLOCK,),
        in_specs=[FIELD_SPEC, ORBITAL_SPEC, ORBITAL_SPEC, RIGHT_SPEC, LEFT_SPEC],
        out_specs=ORBITAL_SPEC,
        out_shape=jax.ShapeDtypeStruct(CUBE, F32),
        compiler_params=PARAMS,
        name="backward",
    )(field, first, second, right, left)


def exchanged_slabs(slab):
    pairs = []
    for pair in range(16):
        for core in range(2):
            for place in range(16):
                pairs.append(((pair * 2 + core) * 16 + place, (place * 2 + core) * 16 + pair))
    return lax.ppermute(slab, AXES, pairs)


def gathered(block, axis):
    return lax.all_gather(block, axis, axis=0, tiled=True)


def body(orbitals):
    slab = pack(orbitals.reshape(SLAB, NG, NG)).reshape(SLAB * PACKED, LANES)
    right = jnp.asarray(right_table())
    left = jnp.asarray(left_table())
    kernel = kernel_table()
    visiting = exchanged_slabs(slab)
    pair = gathered(slab, "zl")
    pair, visiting = lax.optimization_barrier((pair, visiting))
    own = gathered(pair, "y").reshape(CUBE)
    over_zh = gathered(visiting[None], "zh")
    half = SLAB * PACKED // 2
    parts = [gathered(over_zh[None, :, at * half : (at + 1) * half], "x") for at in range(2)]
    first = jnp.stack(parts, axis=2)
    first = first.transpose(1, 0, 2, 3, 4).reshape(CUBE)
    second = lax.ppermute(first, "core", [(0, 1), (1, 0)])
    field = forward(own, first, second, right, left)
    field = middle(field, kernel, left)
    terms = backward(field, first, second, right, left).reshape(NG * PACKED, LANES)
    both = lax.psum_scatter(terms, "y", scatter_dimension=0, tiled=True)
    rows = SLAB * PACKED
    place = lax.axis_index("zl")
    mine = lax.dynamic_slice_in_dim(both, place * rows, rows)
    other = lax.dynamic_slice_in_dim(both, (1 - place) * rows, rows)
    total = mine + lax.ppermute(other, "zl", [(0, 1), (1, 0)])
    return unpack(total.reshape(SLAB, PACKED, LANES)).reshape(orbitals.shape)


def solution(mesh):
    fine = Mesh(mesh.devices.reshape(SIZES), AXES)
    placed = P(BAND, GRID, None)
    return jax.shard_map(
        body, mesh=fine, in_specs=(placed,), out_specs=placed, check_vma=False
    )
```

```python
import math

import jax
import jax.numpy as jnp
import numpy as np
from jax import lax
from jax.experimental import pallas as pl
from jax.experimental.pallas import tpu as pltpu
from jax.sharding import Mesh
from jax.sharding import PartitionSpec as P

MIXING = 0.25
SPACING = 0.31
SCREENING = 0.106

NG = 96
LANES = 128
SLAB = 6
BF16 = jnp.bfloat16
F32 = jnp.float32
AXES = ("zh", "x", "core", "y", "zl")
SIZES = (4, 4, 2, 8, 2)
BAND = ("zh", "x", "core")
GRID = ("y", "zl")
BLOCK = 24
BATCH = 24
PITCH = NG + 8
UNROLL = 1


def cas_halves():
    index = np.arange(NG)
    phases = (index[:, None] * index[None, :] % NG) * (2.0 * math.pi / NG)
    table = np.cos(phases) + np.sin(phases)
    high = table.astype(BF16)
    low = (table - high.astype(np.float64)).astype(BF16)
    return high, low


def right_table():
    high, low = cas_halves()
    table = np.zeros((2 * LANES, 2 * LANES), BF16)
    for row in (0, LANES):
        table[row : row + NG, 0:NG] = high
        table[row : row + NG, LANES : LANES + NG] = low
    return table


def left_table():
    high, low = cas_halves()
    return np.concatenate(
        [np.concatenate([high, high], axis=1), np.concatenate([low, low], axis=1)], axis=0
    )


def kernel_table():
    index = jnp.arange(NG, dtype=jnp.int32)
    signed = jnp.where(index * 2 < NG, index, index - NG).astype(F32)
    wave = signed * (2.0 * math.pi / (NG * SPACING))
    wave_z = jnp.pad(wave, (0, LANES - NG))
    square = (
        (wave * wave)[:, None, None] + (wave * wave)[None, :, None] + (wave_z * wave_z)[None, None, :]
    )
    safe = jnp.where(square > 0, square, 1.0)
    values = 4.0 * math.pi * (1.0 - jnp.exp(-safe / (4.0 * SCREENING * SCREENING))) / safe
    return jnp.where(square > 0, values, 0.0) * (-MIXING / float(NG) ** 3)


def halves(values):
    high = values.astype(BF16)
    low = (values - high.astype(F32)).astype(BF16)
    return high, low


def left_transform(table, columns):
    high, low = halves(columns)
    both = jnp.dot(table, jnp.concatenate([high, low], axis=0), preferred_element_type=F32)
    return both[:NG] + both[NG:]


def right_transform(rows, table):
    high, low = halves(rows)
    both = jnp.dot(jnp.concatenate([high, low], axis=1), table, preferred_element_type=F32)
    return both[:, :LANES] + both[:, LANES:]


PACKED = NG * NG // LANES
TAIL = NG - PACKED
REST = LANES - NG


def pack(planes):
    tail = planes[:, PACKED:]
    thirds = [tail[:, :, REST * at : REST * (at + 1)] for at in range(NG // REST)]
    return jnp.concatenate([planes[:, :PACKED], jnp.concatenate(thirds, axis=1)], axis=2)


def unpack(packed):
    side = packed[:, :, NG:]
    thirds = [side[:, TAIL * at : TAIL * (at + 1)] for at in range(NG // REST)]
    return jnp.concatenate([packed[:, :, :NG], jnp.concatenate(thirds, axis=2)], axis=1)


def lane_mask(rows, low, high):
    lane = lax.broadcasted_iota(jnp.int32, (rows, LANES), 1)
    return (lane >= low) & (lane < high)


def unpack_plane(packed):
    top = jnp.where(lane_mask(PACKED, 0, NG), packed, 0.0)
    tail = jnp.zeros((TAIL, LANES), packed.dtype)
    for at in range(NG // REST):
        rolled = pltpu.roll(packed[TAIL * at : TAIL * (at + 1)], REST * (at + 1), 1)
        tail = jnp.where(lane_mask(TAIL, REST * at, REST * (at + 1)), rolled, tail)
    return jnp.concatenate([top, tail], axis=0)


def pack_plane(plane):
    tail = plane[PACKED:]
    sides = [pltpu.roll(tail, LANES - REST * (at + 1), 1) for at in range(NG // REST)]
    return jnp.where(lane_mask(PACKED, 0, NG), plane[:PACKED], jnp.concatenate(sides, axis=0))


def place(pair, plane):
    return pl.ds(pl.multiple_of((pair * NG + plane) * PITCH, 8), NG)


def line(pair, ky):
    return pl.ds(pair * NG * PITCH + ky, NG, stride=PITCH)


def side_by_side(tiles):
    return jnp.concatenate(tiles, axis=1)


def stacked(tiles):
    return jnp.concatenate(tiles, axis=0)


def lane_tiles(wide):
    return [wide[:, at : at + LANES] for at in range(0, wide.shape[1], LANES)]


def row_tiles(tall):
    return [tall[at : at + NG] for at in range(0, tall.shape[0], NG)]


def pairs_kernel(own_ref, first_ref, second_ref, kernel_ref, right_ref, left_ref, out_ref, field):
    step = pl.program_id(0)
    steps = NG // BLOCK
    right = right_ref[...]
    left = left_ref[...]

    @pl.when(step < steps)
    def forward():
        @pl.loop(0, BLOCK // BATCH, unroll=UNROLL)
        def _(group):
            rows = []
            for at in range(BATCH):
                plane = group * BATCH + at
                own = own_ref[plane].astype(F32)
                rows.append(unpack_plane(own * first_ref[plane].astype(F32)))
                rows.append(unpack_plane(own * second_ref[plane].astype(F32)))
            rows = right_transform(stacked(rows), right)
            columns = left_transform(left, side_by_side(row_tiles(rows)))
            for at, tile in enumerate(lane_tiles(columns)):
                plane = step * BLOCK + group * BATCH + at // 2
                field[place(at % 2, plane), :] = tile

    @pl.when((step >= steps) & (step < 2 * steps))
    def middle():
        @pl.loop(0, BLOCK // BATCH, unroll=UNROLL)
        def _(group):
            base = (step - steps) * BLOCK + group * BATCH
            lines = [line(at % 2, base + at // 2) for at in range(2 * BATCH)]
            columns = left_transform(left, side_by_side([field[at, :] for at in lines]))
            weights = [kernel_ref[group * BATCH + at // 2] for at in range(2 * BATCH)]
            columns = left_transform(left, columns * side_by_side(weights))
            for at, tile in zip(lines, lane_tiles(columns), strict=True):
                field[at, :] = tile

    @pl.when(step >= 2 * steps)
    def backward():
        @pl.loop(0, BLOCK // BATCH, unroll=UNROLL)
        def _(group):
            base = (step - 2 * steps) * BLOCK + group * BATCH
            tiles = [field[place(at % 2, base + at // 2), :] for at in range(2 * BATCH)]
            columns = left_transform(left, side_by_side(tiles))
            tiles = row_tiles(right_transform(stacked(lane_tiles(columns)), right))
            for at in range(BATCH):
                plane = group * BATCH + at
                first = pack_plane(tiles[2 * at]) * first_ref[plane].astype(F32)
                second = pack_plane(tiles[2 * at + 1]) * second_ref[plane].astype(F32)
                out_ref[plane] = first + second


CUBE = (NG, PACKED, LANES)


def pair_terms(own, first, second, kernel, right, left):
    steps = NG // BLOCK

    def clipped(i, low):
        return jnp.clip(i - low, 0, steps - 1)

    def both(i):
        return jnp.where(i < steps, i, clipped(i, 2 * steps))

    def planes(place_of):
        return pl.BlockSpec((BLOCK, PACKED, LANES), lambda i: (place_of(i), 0, 0))

    return pl.pallas_call(
        pairs_kernel,
        grid=(3 * steps,),
        in_specs=[
            planes(lambda i: clipped(i, 0)),
            planes(both),
            planes(both),
            pl.BlockSpec((BLOCK, NG, LANES), lambda i: (clipped(i, steps), 0, 0)),
            pl.BlockSpec((2 * LANES, 2 * LANES), lambda i: (0, 0)),
            pl.BlockSpec((2 * NG, 2 * NG), lambda i: (0, 0)),
        ],
        out_specs=planes(lambda i: clipped(i, 2 * steps)),
        out_shape=jax.ShapeDtypeStruct(CUBE, F32),
        scratch_shapes=[pltpu.VMEM((2 * NG * PITCH, LANES), F32)],
        compiler_params=pltpu.CompilerParams(vmem_limit_bytes=58 * 1024 * 1024),
        cost_estimate=pl.CostEstimate(
            flops=2 * 6 * 2 * NG * NG * 256 * 256, bytes_accessed=17_000_000, transcendentals=0
        ),
        name="pair_terms",
    )(own, first, second, kernel, right, left)


def exchanged_slabs(slab):
    pairs = []
    for pair in range(16):
        for core in range(2):
            for place in range(16):
                pairs.append(((pair * 2 + core) * 16 + place, (place * 2 + core) * 16 + pair))
    return lax.ppermute(slab, AXES, pairs)


def gathered(block, axis):
    return lax.all_gather(block, axis, axis=0, tiled=True)


def body(orbitals):
    slab = pack(orbitals.reshape(SLAB, NG, NG)).reshape(SLAB * PACKED, LANES)
    right = jnp.asarray(right_table())
    left = jnp.asarray(left_table())
    kernel = kernel_table()
    visiting = exchanged_slabs(slab)
    pair = gathered(slab, "zl")
    pair, visiting = lax.optimization_barrier((pair, visiting))
    own = gathered(pair, "y").reshape(CUBE)
    over_zh = gathered(visiting[None], "zh")
    half = SLAB * PACKED // 2
    parts = [gathered(over_zh[None, :, at * half : (at + 1) * half], "x") for at in range(2)]
    first = jnp.stack(parts, axis=2)
    first = first.transpose(1, 0, 2, 3, 4).reshape(CUBE)
    second = lax.ppermute(first, "core", [(0, 1), (1, 0)])
    terms = pair_terms(own, first, second, kernel, right, left).reshape(NG * PACKED, LANES)
    both = lax.psum_scatter(terms, "y", scatter_dimension=0, tiled=True)
    rows = SLAB * PACKED
    place = lax.axis_index("zl")
    mine = lax.dynamic_slice_in_dim(both, place * rows, rows)
    other = lax.dynamic_slice_in_dim(both, (1 - place) * rows, rows)
    total = mine + lax.ppermute(other, "zl", [(0, 1), (1, 0)])
    return unpack(total.reshape(SLAB, PACKED, LANES)).reshape(orbitals.shape)


def solution(mesh):
    fine = Mesh(mesh.devices.reshape(SIZES), AXES)
    placed = P(BAND, GRID, None)
    return jax.shard_map(
        body, mesh=fine, in_specs=(placed,), out_specs=placed, check_vma=False
    )
```

```python
import functools
import math

import jax
import jax.numpy as jnp
import numpy as np
from jax import lax
from jax.experimental import pallas as pl
from jax.experimental.pallas import tpu as pltpu
from jax.sharding import Mesh
from jax.sharding import PartitionSpec as P

MIXING = 0.25
SPACING = 0.31
SCREENING = 0.106

NG = 96
LANES = 128
SLAB = 6
BF16 = jnp.bfloat16
F32 = jnp.float32
AXES = ("zh", "x", "core", "y", "zl")
SIZES = (4, 4, 2, 8, 2)
BAND = ("zh", "x", "core")
GRID = ("y", "zl")
BATCH = 24
SLABS = BATCH // SLAB
VMEM_MIB = 58
PITCH = NG + 8
UNROLL = 1


def cas_halves():
    index = np.arange(NG)
    phases = (index[:, None] * index[None, :] % NG) * (2.0 * math.pi / NG)
    table = np.cos(phases) + np.sin(phases)
    high = table.astype(BF16)
    low = (table - high.astype(np.float64)).astype(BF16)
    return high, low


def right_table():
    high, low = cas_halves()
    table = np.zeros((2 * LANES, 2 * LANES), BF16)
    for row in (0, LANES):
        table[row : row + NG, 0:NG] = high
        table[row : row + NG, LANES : LANES + NG] = low
    return table


def left_table():
    high, low = cas_halves()
    return np.concatenate(
        [np.concatenate([high, high], axis=1), np.concatenate([low, low], axis=1)], axis=0
    )


def kernel_table(index):
    signed = jnp.where(index * 2 < NG, index, index - NG).astype(F32)
    wave = signed * (2.0 * math.pi / (NG * SPACING))
    wave_z = jnp.pad(wave, (0, LANES - NG))
    square = (
        (wave * wave)[:, None, None] + (wave * wave)[None, :, None] + (wave_z * wave_z)[None, None, :]
    )
    safe = jnp.where(square > 0, square, 1.0)
    values = 4.0 * math.pi * (1.0 - jnp.exp(-safe / (4.0 * SCREENING * SCREENING))) / safe
    return jnp.where(square > 0, values, 0.0) * (-MIXING / float(NG) ** 3)


def halves(values):
    high = values.astype(BF16)
    low = (values - high.astype(F32)).astype(BF16)
    return high, low


def left_transform(table, columns):
    high, low = halves(columns)
    both = jnp.dot(table, jnp.concatenate([high, low], axis=0), preferred_element_type=F32)
    return both[:NG] + both[NG:]


def right_transform(rows, table):
    high, low = halves(rows)
    both = jnp.dot(jnp.concatenate([high, low], axis=1), table, preferred_element_type=F32)
    return both[:, :LANES] + both[:, LANES:]


PACKED = NG * NG // LANES
TAIL = NG - PACKED
REST = LANES - NG


def pack(planes):
    tail = planes[:, PACKED:]
    thirds = [tail[:, :, REST * at : REST * (at + 1)] for at in range(NG // REST)]
    return jnp.concatenate([planes[:, :PACKED], jnp.concatenate(thirds, axis=1)], axis=2)


def unpack(packed):
    side = packed[:, :, NG:]
    thirds = [side[:, TAIL * at : TAIL * (at + 1)] for at in range(NG // REST)]
    return jnp.concatenate([packed[:, :, :NG], jnp.concatenate(thirds, axis=2)], axis=1)


def lane_mask(rows, low, high):
    lane = lax.broadcasted_iota(jnp.int32, (rows, LANES), 1)
    return (lane >= low) & (lane < high)


def unpack_plane(packed):
    top = jnp.where(lane_mask(PACKED, 0, NG), packed, 0.0)
    tail = jnp.zeros((TAIL, LANES), packed.dtype)
    for at in range(NG // REST):
        rolled = pltpu.roll(packed[TAIL * at : TAIL * (at + 1)], REST * (at + 1), 1)
        tail = jnp.where(lane_mask(TAIL, REST * at, REST * (at + 1)), rolled, tail)
    return jnp.concatenate([top, tail], axis=0)


def pack_plane(plane):
    tail = plane[PACKED:]
    sides = [pltpu.roll(tail, LANES - REST * (at + 1), 1) for at in range(NG // REST)]
    return jnp.where(lane_mask(PACKED, 0, NG), plane[:PACKED], jnp.concatenate(sides, axis=0))


def place(pair, plane):
    return pl.ds(pl.multiple_of((pair * NG + plane) * PITCH, 8), NG)


def line(pair, ky):
    return pl.ds(pair * NG * PITCH + ky, NG, stride=PITCH)


def side_by_side(tiles):
    return jnp.concatenate(tiles, axis=1)


def stacked(tiles):
    return jnp.concatenate(tiles, axis=0)


def lane_tiles(wide):
    return [wide[:, at : at + LANES] for at in range(0, wide.shape[1], LANES)]


def row_tiles(tall):
    return [tall[at : at + NG] for at in range(0, tall.shape[0], NG)]


def pairs_kernel(order_ref, own_ref, *refs):
    *visitor_refs, kernel_ref, right_ref, left_ref, out_ref, field = refs
    step = pl.program_id(0)
    steps = NG // BATCH
    right = right_ref[...]
    left = left_ref[...]

    def visitor(pair, plane):
        slab = lax.rem(plane // SLAB + order_ref[pair, steps], SLABS)
        return visitor_refs[pair][slab * SLAB + plane % SLAB].astype(F32)

    @pl.when(step < steps)
    def forward():
        rows = []
        for at in range(BATCH):
            own = own_ref[at].astype(F32)
            rows += [unpack_plane(own * visitor(pair, at)) for pair in range(2)]
        rows = right_transform(stacked(rows), right)
        columns = left_transform(left, side_by_side(row_tiles(rows)))
        for at, tile in enumerate(lane_tiles(columns)):
            field[place(at % 2, step * BATCH + at // 2), :] = tile

    @pl.when((step >= steps) & (step < 2 * steps))
    def middle():
        first = (step - steps) * BATCH
        lines = [line(at % 2, first + at // 2) for at in range(2 * BATCH)]
        columns = left_transform(left, side_by_side([field[at, :] for at in lines]))
        columns = columns * side_by_side([kernel_ref[at // 2] for at in range(2 * BATCH)])
        columns = left_transform(left, columns)
        for at, tile in zip(lines, lane_tiles(columns), strict=True):
            field[at, :] = tile

    @pl.when(step >= 2 * steps)
    def backward():
        first = (step - 2 * steps) * BATCH
        tiles = [field[place(at % 2, first + at // 2), :] for at in range(2 * BATCH)]
        columns = left_transform(left, side_by_side(tiles))
        tiles = row_tiles(right_transform(stacked(lane_tiles(columns)), right))
        for at in range(BATCH):
            terms = [pack_plane(tiles[2 * at + pair]) * visitor(pair, at) for pair in range(2)]
            out_ref[at] = terms[0] + terms[1]


CUBE = (NG, PACKED, LANES)


def pair_terms(order, own, first, second, kernel, right, left):
    steps = NG // BATCH

    def clipped(i, low):
        return jnp.clip(i - low, 0, steps - 1)

    def both(i):
        return jnp.where(i < steps, i, clipped(i, 2 * steps))

    def planes(count, place_of):
        return pl.BlockSpec((count, PACKED, LANES), lambda i, order: (place_of(i, order), 0, 0))

    def visitor(pair):
        return planes(BATCH, lambda i, order: order[pair, both(i)])

    return pl.pallas_call(
        pairs_kernel,
        grid_spec=pltpu.PrefetchScalarGridSpec(
            num_scalar_prefetch=1,
            grid=(3 * steps,),
            in_specs=[
                planes(BATCH, lambda i, order: clipped(i, 0)),
                visitor(0),
                visitor(1),
                pl.BlockSpec((BATCH, NG, LANES), lambda i, order: (clipped(i, steps), 0, 0)),
                pl.BlockSpec((2 * LANES, 2 * LANES), lambda i, order: (0, 0)),
                pl.BlockSpec((2 * NG, 2 * NG), lambda i, order: (0, 0)),
            ],
            out_specs=planes(BATCH, lambda i, order: clipped(i, 2 * steps)),
            scratch_shapes=[pltpu.VMEM((2 * NG * PITCH, LANES), F32)],
        ),
        out_shape=jax.ShapeDtypeStruct(CUBE, F32),
        compiler_params=pltpu.CompilerParams(vmem_limit_bytes=VMEM_MIB * 1024 * 1024),
        cost_estimate=pl.CostEstimate(
            flops=4 * 6 * NG * NG * 256 * 256, bytes_accessed=17_000_000, transcendentals=0
        ),
        name="pair_terms",
    )(order, own, first, second, kernel, right, left)


def meeting_place(zh, x, core):
    return (zh + 4 * ((x % 2 + core) % 2)) % 8, x // 2


def landing(zh, x, y, zl, meeting_y):
    apart = (y - meeting_y // 2 * 2) % 8
    return (zh + 2 * (apart % 2) + zl) % 4, (x + apart // 2) % 4


def exchanged_slabs(slab):
    pairs = []
    for zh, x, core, y, zl in np.ndindex(*SIZES):
        there_y, there_zl = meeting_place(zh, x, core)
        there_zh, there_x = landing(zh, x, y, zl, there_y)
        target = (there_zh, there_x, core, there_y, there_zl)
        pairs.append(
            (int(np.ravel_multi_index((zh, x, core, y, zl), SIZES)), int(np.ravel_multi_index(target, SIZES)))
        )
    return lax.ppermute(slab, AXES, pairs)


def visiting_order(core):
    y, zl = lax.axis_index("y"), lax.axis_index("zl")
    zh = y % 4
    x = 2 * zl + (y // 4 + core) % 2
    block = jnp.arange(4, dtype=jnp.int32)
    apart = (x + block - y // 2 - lax.axis_index("x")) % 4
    place = jnp.where(apart == 3, 1, jnp.where(apart == 0, 0, apart + 1))
    return jnp.concatenate([place, zh[None]]).astype(jnp.int32)


def gathered_x(block):
    def shifted(part, by):
        return lax.ppermute(part, "x", [(at, (at + by) % 4) for at in range(4)])

    before, after = shifted(block, 1), shifted(block, 3)
    return [block, before, after, shifted(before[:2], 1), shifted(after[2:], 3)]


def gathered(block, axis):
    return lax.all_gather(block, axis, axis=0, tiled=True)


def body(orbitals):
    slab = pack(orbitals.reshape(SLAB, NG, NG)).reshape(SLAB * PACKED, LANES)
    right = jnp.asarray(right_table())
    left = jnp.asarray(left_table())
    visiting = exchanged_slabs(slab)
    pair = gathered(slab, "zl")
    pair, visiting = lax.optimization_barrier((pair, visiting))
    own = gathered(pair, "y").reshape(CUBE)
    blocks = gathered_x(gathered(visiting[None], "zh"))
    index = jnp.arange(NG, dtype=jnp.int32)
    own, index, *blocks = lax.optimization_barrier((own, index, *blocks))
    kernel = kernel_table(index)
    first = jnp.concatenate(blocks).reshape(CUBE)
    second = lax.ppermute(first, "core", [(0, 1), (1, 0)])
    core = lax.axis_index("core")
    order = jnp.stack([visiting_order(core), visiting_order(1 - core)])
    terms = pair_terms(order, own, first, second, kernel, right, left)
    both = lax.psum_scatter(terms.reshape(NG * PACKED, LANES), "y", scatter_dimension=0, tiled=True)
    rows = SLAB * PACKED
    place = lax.axis_index("zl")
    mine = lax.dynamic_slice_in_dim(both, place * rows, rows)
    other = lax.dynamic_slice_in_dim(both, (1 - place) * rows, rows)
    total = mine + lax.ppermute(other, "zl", [(0, 1), (1, 0)])
    return unpack(total.reshape(SLAB, PACKED, LANES)).reshape(orbitals.shape)


def solution(mesh):
    fine = Mesh(mesh.devices.reshape(SIZES), AXES)
    placed = P(BAND, GRID, None)
    return jax.shard_map(
        body, mesh=fine, in_specs=(placed,), out_specs=placed, check_vma=False
    )
```

```python
import functools
import math

import jax
import jax.numpy as jnp
import numpy as np
from jax import lax
from jax.experimental import pallas as pl
from jax.experimental.pallas import tpu as pltpu
from jax.sharding import Mesh
from jax.sharding import PartitionSpec as P

MIXING = 0.25
SPACING = 0.31
SCREENING = 0.106

NG = 96
LANES = 128
SLAB = 6
BF16 = jnp.bfloat16
F32 = jnp.float32
AXES = ("zh", "x", "core", "y", "zl")
SIZES = (4, 4, 2, 8, 2)
BAND = ("zh", "x", "core")
GRID = ("y", "zl")
BATCH = 24
SLABS = BATCH // SLAB
VMEM_MIB = 58
NEAR = 4
FAR = SLAB - NEAR
PITCH = NG + 8
UNROLL = 1


def cas_halves():
    index = np.arange(NG)
    phases = (index[:, None] * index[None, :] % NG) * (2.0 * math.pi / NG)
    table = np.cos(phases) + np.sin(phases)
    high = table.astype(BF16)
    low = (table - high.astype(np.float64)).astype(BF16)
    return high, low


def right_table():
    high, low = cas_halves()
    table = np.zeros((2 * LANES, 2 * LANES), BF16)
    for row in (0, LANES):
        table[row : row + NG, 0:NG] = high
        table[row : row + NG, LANES : LANES + NG] = low
    return table


def left_table():
    high, low = cas_halves()
    return np.concatenate(
        [np.concatenate([high, high], axis=1), np.concatenate([low, low], axis=1)], axis=0
    )


def kernel_table(index):
    signed = jnp.where(index * 2 < NG, index, index - NG).astype(F32)
    wave = signed * (2.0 * math.pi / (NG * SPACING))
    wave_z = jnp.pad(wave, (0, LANES - NG))
    square = (
        (wave * wave)[: NG // 2 + 1, None, None] + (wave * wave)[None, :, None] + (wave_z * wave_z)[None, None, :]
    )
    safe = jnp.where(square > 0, square, 1.0)
    values = 4.0 * math.pi * (1.0 - jnp.exp(-safe / (4.0 * SCREENING * SCREENING))) / safe
    return jnp.where(square > 0, values, 0.0) * (-MIXING / float(NG) ** 3)


def halves(values):
    high = values.astype(BF16)
    low = (values - high.astype(F32)).astype(BF16)
    return high, low


def left_transform(table, columns):
    high, low = halves(columns)
    both = jnp.dot(table, jnp.concatenate([high, low], axis=0), preferred_element_type=F32)
    return both[:NG] + both[NG:]


def right_transform(rows, table):
    high, low = halves(rows)
    both = jnp.dot(jnp.concatenate([high, low], axis=1), table, preferred_element_type=F32)
    return both[:, :LANES] + both[:, LANES:]


PACKED = NG * NG // LANES
TAIL = NG - PACKED
REST = LANES - NG


def pack(planes):
    tail = planes[:, PACKED:]
    thirds = [tail[:, :, REST * at : REST * (at + 1)] for at in range(NG // REST)]
    return jnp.concatenate([planes[:, :PACKED], jnp.concatenate(thirds, axis=1)], axis=2)


def unpack(packed):
    side = packed[:, :, NG:]
    thirds = [side[:, TAIL * at : TAIL * (at + 1)] for at in range(NG // REST)]
    return jnp.concatenate([packed[:, :, :NG], jnp.concatenate(thirds, axis=2)], axis=1)


def lane_mask(rows, low, high):
    lane = lax.broadcasted_iota(jnp.int32, (rows, LANES), 1)
    return (lane >= low) & (lane < high)


def unpack_plane(packed):
    top = jnp.where(lane_mask(PACKED, 0, NG), packed, 0.0)
    tail = jnp.zeros((TAIL, LANES), packed.dtype)
    for at in range(NG // REST):
        rolled = pltpu.roll(packed[TAIL * at : TAIL * (at + 1)], REST * (at + 1), 1)
        tail = jnp.where(lane_mask(TAIL, REST * at, REST * (at + 1)), rolled, tail)
    return jnp.concatenate([top, tail], axis=0)


def pack_plane(plane):
    tail = plane[PACKED:]
    sides = [pltpu.roll(tail, LANES - REST * (at + 1), 1) for at in range(NG // REST)]
    return jnp.where(lane_mask(PACKED, 0, NG), plane[:PACKED], jnp.concatenate(sides, axis=0))


def place(pair, plane):
    return pl.ds(pl.multiple_of((pair * NG + plane) * PITCH, 8), NG)


def line(pair, ky):
    return pl.ds(pair * NG * PITCH + ky, NG, stride=PITCH)


def side_by_side(tiles):
    return jnp.concatenate(tiles, axis=1)


def stacked(tiles):
    return jnp.concatenate(tiles, axis=0)


def lane_tiles(wide):
    return [wide[:, at : at + LANES] for at in range(0, wide.shape[1], LANES)]


def row_tiles(tall):
    return [tall[at : at + NG] for at in range(0, tall.shape[0], NG)]


def pairs_kernel(order_ref, own_ref, *refs):
    *visitor_refs, right_ref, left_ref, kernel_ref, near_ref, far_ref, field, weights, arrived = refs
    weights_copy = pltpu.make_async_copy(kernel_ref, weights, arrived)
    step = pl.program_id(0)
    steps = NG // BATCH
    right = right_ref[...]
    left = left_ref[...]

    def visitor(pair, plane):
        slab = lax.rem(plane // SLAB + order_ref[pair, steps], SLABS)
        return visitor_refs[pair][slab * SLAB + plane % SLAB].astype(F32)

    @pl.when(step == 0)
    def fetch():
        weights_copy.start()

    @pl.when(step == steps)
    def fetched():
        weights_copy.wait()

    @pl.when(step < steps)
    def forward():
        rows = []
        for at in range(BATCH):
            own = own_ref[at].astype(F32)
            rows += [unpack_plane(own * visitor(pair, at)) for pair in range(2)]
        rows = right_transform(stacked(rows), right)
        columns = left_transform(left, side_by_side(row_tiles(rows)))
        for at, tile in enumerate(lane_tiles(columns)):
            field[place(at % 2, step * BATCH + at // 2), :] = tile

    @pl.when((step >= steps) & (step < 2 * steps))
    def middle():
        first = (step - steps) * BATCH
        lines = [line(at % 2, first + at // 2) for at in range(2 * BATCH)]
        columns = left_transform(left, side_by_side([field[at, :] for at in lines]))
        rows = [jnp.minimum(first + at, NG - first - at) for at in range(BATCH)]
        columns = columns * side_by_side([weights[rows[at // 2]] for at in range(2 * BATCH)])
        columns = left_transform(left, columns)
        for at, tile in zip(lines, lane_tiles(columns), strict=True):
            field[at, :] = tile

    @pl.when(step >= 2 * steps)
    def backward():
        first = (step - 2 * steps) * BATCH
        tiles = [field[place(at % 2, first + at // 2), :] for at in range(2 * BATCH)]
        columns = left_transform(left, side_by_side(tiles))
        tiles = row_tiles(right_transform(stacked(lane_tiles(columns)), right))
        for at in range(BATCH):
            terms = [pack_plane(tiles[2 * at + pair]) * visitor(pair, at) for pair in range(2)]
            slab, plane = divmod(at, SLAB)
            if plane < NEAR:
                near_ref[slab * NEAR + plane] = terms[0] + terms[1]
            else:
                far_ref[slab * FAR + plane - NEAR] = terms[0] + terms[1]


CUBE = (NG, PACKED, LANES)


def pair_terms(order, own, first, second, kernel, right, left):
    steps = NG // BATCH

    def clipped(i, low):
        return jnp.clip(i - low, 0, steps - 1)

    def both(i):
        return jnp.where(i < steps, i, clipped(i, 2 * steps))

    def planes(count, place_of):
        return pl.BlockSpec((count, PACKED, LANES), lambda i, order: (place_of(i, order), 0, 0))

    def visitor(pair):
        return planes(BATCH, lambda i, order: order[pair, both(i)])

    return pl.pallas_call(
        pairs_kernel,
        grid_spec=pltpu.PrefetchScalarGridSpec(
            num_scalar_prefetch=1,
            grid=(3 * steps,),
            in_specs=[
                planes(BATCH, lambda i, order: clipped(i, 0)),
                visitor(0),
                visitor(1),
                pl.BlockSpec((2 * LANES, 2 * LANES), lambda i, order: (0, 0)),
                pl.BlockSpec((2 * NG, 2 * NG), lambda i, order: (0, 0)),
                pl.BlockSpec(memory_space=pl.ANY),
            ],
            out_specs=[
                planes(count * SLABS, lambda i, order: clipped(i, 2 * steps)) for count in (NEAR, FAR)
            ],
            scratch_shapes=[
                pltpu.VMEM((2 * NG * PITCH, LANES), F32),
                pltpu.VMEM((NG // 2 + 1, NG, LANES), F32),
                pltpu.SemaphoreType.DMA,
            ],
        ),
        out_shape=[
            jax.ShapeDtypeStruct((NG // SLAB * count, PACKED, LANES), F32) for count in (NEAR, FAR)
        ],
        compiler_params=pltpu.CompilerParams(vmem_limit_bytes=VMEM_MIB * 1024 * 1024),
        cost_estimate=pl.CostEstimate(
            flops=4 * 6 * NG * NG * 256 * 256, bytes_accessed=17_000_000, transcendentals=0
        ),
        name="pair_terms",
    )(order, own, first, second, right, left, kernel)


def meeting_place(zh, x, core):
    return (zh + 4 * ((x % 2 + core) % 2)) % 8, x // 2


def landing(zh, x, y, zl, meeting_y):
    apart = (y - meeting_y // 2 * 2) % 8
    return (zh + 2 * (apart % 2) + zl) % 4, (x + apart // 2) % 4


def exchanged_slabs(slab):
    pairs = []
    for zh, x, core, y, zl in np.ndindex(*SIZES):
        there_y, there_zl = meeting_place(zh, x, core)
        there_zh, there_x = landing(zh, x, y, zl, there_y)
        target = (there_zh, there_x, core, there_y, there_zl)
        pairs.append(
            (int(np.ravel_multi_index((zh, x, core, y, zl), SIZES)), int(np.ravel_multi_index(target, SIZES)))
        )
    return lax.ppermute(slab, AXES, pairs)


def visiting_order(core):
    y, zl = lax.axis_index("y"), lax.axis_index("zl")
    zh = y % 4
    x = 2 * zl + (y // 4 + core) % 2
    block = jnp.arange(4, dtype=jnp.int32)
    apart = (x + block - y // 2 - lax.axis_index("x")) % 4
    place = jnp.where(apart == 3, 1, jnp.where(apart == 0, 0, apart + 1))
    return jnp.concatenate([place, zh[None]]).astype(jnp.int32)


def gathered_x(block):
    def shifted(part, by):
        return lax.ppermute(part, "x", [(at, (at + by) % 4) for at in range(4)])

    before, after = shifted(block, 1), shifted(block, 3)
    return [block, before, after, shifted(before[:2], 1), shifted(after[2:], 3)]


def gathered(block, axis):
    return lax.all_gather(block, axis, axis=0, tiled=True)


def scattered(terms):
    return lax.psum_scatter(terms, "y", scatter_dimension=0, tiled=True)


def both_places(slabs):
    place = lax.axis_index("zl")
    mine = lax.dynamic_index_in_dim(slabs, place, keepdims=False)
    other = lax.dynamic_index_in_dim(slabs, 1 - place, keepdims=False)
    return mine + lax.ppermute(other, "zl", [(0, 1), (1, 0)])


def body(orbitals):
    slab = pack(orbitals.reshape(SLAB, NG, NG)).reshape(SLAB * PACKED, LANES)
    right = jnp.asarray(right_table())
    left = jnp.asarray(left_table())
    visiting = exchanged_slabs(slab)
    pair = gathered(slab, "zl")
    pair, visiting = lax.optimization_barrier((pair, visiting))
    own = gathered(pair, "y").reshape(CUBE)
    blocks = gathered_x(gathered(visiting[None], "zh"))
    index = jnp.arange(NG, dtype=jnp.int32)
    own, index, *blocks = lax.optimization_barrier((own, index, *blocks))
    kernel = kernel_table(index)
    first = jnp.concatenate(blocks).reshape(CUBE)
    second = lax.ppermute(first, "core", [(0, 1), (1, 0)])
    core = lax.axis_index("core")
    order = jnp.stack([visiting_order(core), visiting_order(1 - core)])
    near, far = pair_terms(order, own, first, second, kernel, right, left)
    near = scattered(near.reshape(-1, LANES)).reshape(2, NEAR, PACKED, LANES)
    far = scattered(far.reshape(-1, 8 * LANES)).reshape(2, FAR, PACKED, LANES)
    total = jnp.concatenate([both_places(near), both_places(far)])
    return unpack(total).reshape(orbitals.shape)


def solution(mesh):
    fine = Mesh(mesh.devices.reshape(SIZES), AXES)
    placed = P(BAND, GRID, None)
    return jax.shard_map(
        body, mesh=fine, in_specs=(placed,), out_specs=placed, check_vma=False
    )
```

```python
import functools
import math

import jax
import jax.numpy as jnp
import numpy as np
from jax import lax
from jax.experimental import pallas as pl
from jax.experimental.pallas import tpu as pltpu
from jax.sharding import Mesh
from jax.sharding import PartitionSpec as P

MIXING = 0.25
SPACING = 0.31
SCREENING = 0.106

NG = 96
LANES = 128
SLAB = 6
BF16 = jnp.bfloat16
F32 = jnp.float32
AXES = ("zh", "x", "core", "y", "zl")
SIZES = (4, 4, 2, 8, 2)
BAND = ("zh", "x", "core")
GRID = ("y", "zl")
BATCH = 24
SLABS = BATCH // SLAB
VMEM_MIB = 50
NEAR = 4
FAR = SLAB - NEAR
PITCH = NG + 8
UNROLL = 1


def cas_halves():
    index = np.arange(NG)
    phases = (index[:, None] * index[None, :] % NG) * (2.0 * math.pi / NG)
    table = np.cos(phases) + np.sin(phases)
    high = table.astype(BF16)
    low = (table - high.astype(np.float64)).astype(BF16)
    return high, low


def right_table():
    high, low = cas_halves()
    table = np.zeros((2 * LANES, 2 * LANES), BF16)
    for row in (0, LANES):
        table[row : row + NG, 0:NG] = high
        table[row : row + NG, LANES : LANES + NG] = low
    return table


def left_table():
    high, low = cas_halves()
    return np.concatenate(
        [np.concatenate([high, high], axis=1), np.concatenate([low, low], axis=1)], axis=0
    )


def kernel_table(index):
    signed = jnp.where(index * 2 < NG, index, index - NG).astype(F32)
    wave = signed * (2.0 * math.pi / (NG * SPACING))
    wave_z = jnp.pad(wave, (0, LANES - NG))
    square = (
        (wave * wave)[: NG // 2 + 1, None, None] + (wave * wave)[None, :, None] + (wave_z * wave_z)[None, None, :]
    )
    safe = jnp.where(square > 0, square, 1.0)
    values = 4.0 * math.pi * (1.0 - jnp.exp(-safe / (4.0 * SCREENING * SCREENING))) / safe
    return jnp.where(square > 0, values, 0.0) * (-MIXING / float(NG) ** 3)


def halves(values):
    high = values.astype(BF16)
    low = (values - high.astype(F32)).astype(BF16)
    return high, low


def left_transform(table, columns):
    high, low = halves(columns)
    both = jnp.dot(table, jnp.concatenate([high, low], axis=0), preferred_element_type=F32)
    return both[:NG] + both[NG:]


def right_transform(rows, table):
    high, low = halves(rows)
    both = jnp.dot(jnp.concatenate([high, low], axis=1), table, preferred_element_type=F32)
    return both[:, :LANES] + both[:, LANES:]


PACKED = NG * NG // LANES
TAIL = NG - PACKED
REST = LANES - NG


def pack(planes):
    tail = planes[:, PACKED:]
    thirds = [tail[:, :, REST * at : REST * (at + 1)] for at in range(NG // REST)]
    return jnp.concatenate([planes[:, :PACKED], jnp.concatenate(thirds, axis=1)], axis=2)


def unpack(packed):
    side = packed[:, :, NG:]
    thirds = [side[:, TAIL * at : TAIL * (at + 1)] for at in range(NG // REST)]
    return jnp.concatenate([packed[:, :, :NG], jnp.concatenate(thirds, axis=2)], axis=1)


def lane_mask(rows, low, high):
    lane = lax.broadcasted_iota(jnp.int32, (rows, LANES), 1)
    return (lane >= low) & (lane < high)


def unpack_plane(packed):
    top = jnp.where(lane_mask(PACKED, 0, NG), packed, 0.0)
    tail = jnp.zeros((TAIL, LANES), packed.dtype)
    for at in range(NG // REST):
        rolled = pltpu.roll(packed[TAIL * at : TAIL * (at + 1)], REST * (at + 1), 1)
        tail = jnp.where(lane_mask(TAIL, REST * at, REST * (at + 1)), rolled, tail)
    return jnp.concatenate([top, tail], axis=0)


def pack_plane(plane):
    tail = plane[PACKED:]
    sides = [pltpu.roll(tail, LANES - REST * (at + 1), 1) for at in range(NG // REST)]
    return jnp.where(lane_mask(PACKED, 0, NG), plane[:PACKED], jnp.concatenate(sides, axis=0))


def place(pair, plane):
    return pl.ds(pl.multiple_of((pair * NG + plane) * PITCH, 8), NG)


def line(pair, ky):
    return pl.ds(pair * NG * PITCH + ky, NG, stride=PITCH)


def side_by_side(tiles):
    return jnp.concatenate(tiles, axis=1)


def stacked(tiles):
    return jnp.concatenate(tiles, axis=0)


def lane_tiles(wide):
    return [wide[:, at : at + LANES] for at in range(0, wide.shape[1], LANES)]


def row_tiles(tall):
    return [tall[at : at + NG] for at in range(0, tall.shape[0], NG)]


def pairs_kernel(order_ref, own_ref, *refs):
    *visitor_refs, right_ref, left_ref, kernel_ref, near_ref, far_ref, field, weights, arrived = refs
    weights_copy = pltpu.make_async_copy(kernel_ref, weights, arrived)
    step = pl.program_id(0)
    steps = NG // BATCH
    right = right_ref[...]
    left = left_ref[...]

    def visitor(pair, plane):
        slab = lax.rem(plane // SLAB + order_ref[pair, steps], SLABS)
        return visitor_refs[pair][slab * SLAB + plane % SLAB].astype(F32)

    @pl.when(step == 0)
    def fetch():
        weights_copy.start()

    @pl.when(step == steps)
    def fetched():
        weights_copy.wait()

    @pl.when(step < steps)
    def forward():
        rows = []
        for at in range(BATCH):
            own = own_ref[at].astype(F32)
            rows += [unpack_plane(own * visitor(pair, at)) for pair in range(2)]
        rows = right_transform(stacked(rows), right)
        columns = left_transform(left, side_by_side(row_tiles(rows)))
        for at, tile in enumerate(lane_tiles(columns)):
            field[place(at % 2, step * BATCH + at // 2), :] = tile

    @pl.when((step >= steps) & (step < 2 * steps))
    def middle():
        first = (step - steps) * BATCH
        lines = [line(at % 2, first + at // 2) for at in range(2 * BATCH)]
        columns = left_transform(left, side_by_side([field[at, :] for at in lines]))
        rows = [jnp.minimum(first + at, NG - first - at) for at in range(BATCH)]
        columns = columns * side_by_side([weights[rows[at // 2]] for at in range(2 * BATCH)])
        columns = left_transform(left, columns)
        for at, tile in zip(lines, lane_tiles(columns), strict=True):
            field[at, :] = tile

    @pl.when(step >= 2 * steps)
    def backward():
        first = (step - 2 * steps) * BATCH
        tiles = [field[place(at % 2, first + at // 2), :] for at in range(2 * BATCH)]
        columns = left_transform(left, side_by_side(tiles))
        tiles = row_tiles(right_transform(stacked(lane_tiles(columns)), right))
        for at in range(BATCH):
            terms = [pack_plane(tiles[2 * at + pair]) * visitor(pair, at) for pair in range(2)]
            slab, plane = divmod(at, SLAB)
            if plane < NEAR:
                near_ref[slab * NEAR + plane] = terms[0] + terms[1]
            else:
                far_ref[slab * FAR + plane - NEAR] = terms[0] + terms[1]


CUBE = (NG, PACKED, LANES)


def pair_terms(order, own, first, second, kernel, right, left):
    steps = NG // BATCH

    def clipped(i, low):
        return jnp.clip(i - low, 0, steps - 1)

    def both(i):
        return jnp.where(i < steps, i, clipped(i, 2 * steps))

    def planes(count, place_of):
        return pl.BlockSpec((count, PACKED, LANES), lambda i, order: (place_of(i, order), 0, 0))

    def visitor(pair):
        return planes(BATCH, lambda i, order: order[pair, both(i)])

    return pl.pallas_call(
        pairs_kernel,
        grid_spec=pltpu.PrefetchScalarGridSpec(
            num_scalar_prefetch=1,
            grid=(3 * steps,),
            in_specs=[
                planes(BATCH, lambda i, order: clipped(i, 0)),
                visitor(0),
                visitor(1),
                pl.BlockSpec((2 * LANES, 2 * LANES), lambda i, order: (0, 0)),
                pl.BlockSpec((2 * NG, 2 * NG), lambda i, order: (0, 0)),
                pl.BlockSpec(memory_space=pl.ANY),
            ],
            out_specs=[
                planes(count * SLABS, lambda i, order: clipped(i, 2 * steps)) for count in (NEAR, FAR)
            ],
            scratch_shapes=[
                pltpu.VMEM((2 * NG * PITCH, LANES), F32),
                pltpu.VMEM((NG // 2 + 1, NG, LANES), F32),
                pltpu.SemaphoreType.DMA,
            ],
        ),
        out_shape=[
            jax.ShapeDtypeStruct((NG // SLAB * count, PACKED, LANES), F32) for count in (NEAR, FAR)
        ],
        compiler_params=pltpu.CompilerParams(vmem_limit_bytes=VMEM_MIB * 1024 * 1024),
        cost_estimate=pl.CostEstimate(
            flops=4 * 6 * NG * NG * 256 * 256, bytes_accessed=17_000_000, transcendentals=0
        ),
        name="pair_terms",
    )(order, own, first, second, right, left, kernel)


def meeting_place(zh, x, core):
    return (zh + 4 * ((x % 2 + core) % 2)) % 8, x // 2


def landing(zh, x, y, zl, meeting_y):
    apart = (y - meeting_y // 2 * 2) % 8
    return (zh + 2 * (apart % 2) + zl) % 4, (x + apart // 2) % 4


def exchanged_slabs(slab):
    pairs = []
    for zh, x, core, y, zl in np.ndindex(*SIZES):
        there_y, there_zl = meeting_place(zh, x, core)
        there_zh, there_x = landing(zh, x, y, zl, there_y)
        target = (there_zh, there_x, core, there_y, there_zl)
        pairs.append(
            (int(np.ravel_multi_index((zh, x, core, y, zl), SIZES)), int(np.ravel_multi_index(target, SIZES)))
        )
    return lax.ppermute(slab, AXES, pairs)


def visiting_order(core):
    y, zl = lax.axis_index("y"), lax.axis_index("zl")
    zh = y % 4
    x = 2 * zl + (y // 4 + core) % 2
    block = jnp.arange(4, dtype=jnp.int32)
    apart = (x + block - y // 2 - lax.axis_index("x")) % 4
    place = jnp.where(apart == 3, 1, jnp.where(apart == 0, 0, apart + 1))
    return jnp.concatenate([place, zh[None]]).astype(jnp.int32)


def gathered_x(block):
    def shifted(part, by):
        return lax.ppermute(part, "x", [(at, (at + by) % 4) for at in range(4)])

    before, after = shifted(block, 1), shifted(block, 3)
    return [block, before, after, shifted(before[:2], 1), shifted(after[2:], 3)]


def gathered(block, axis):
    return lax.all_gather(block, axis, axis=0, tiled=True)


def scattered(terms):
    return lax.psum_scatter(terms, "y", scatter_dimension=0, tiled=True)


def both_places(slabs):
    place = lax.axis_index("zl")
    mine = lax.dynamic_index_in_dim(slabs, place, keepdims=False)
    other = lax.dynamic_index_in_dim(slabs, 1 - place, keepdims=False)
    return mine + lax.ppermute(other, "zl", [(0, 1), (1, 0)])


def body(orbitals):
    slab = pack(orbitals.reshape(SLAB, NG, NG)).reshape(SLAB * PACKED, LANES)
    right = jnp.asarray(right_table())
    left = jnp.asarray(left_table())
    visiting = exchanged_slabs(slab)
    pair = gathered(slab, "zl")
    pair, visiting = lax.optimization_barrier((pair, visiting))
    own = gathered(pair, "y").reshape(CUBE)
    blocks = gathered_x(gathered(visiting[None], "zh"))
    index = jnp.arange(NG, dtype=jnp.int32)
    own, index, *blocks = lax.optimization_barrier((own, index, *blocks))
    kernel = kernel_table(index)
    first = jnp.concatenate(blocks).reshape(CUBE)
    second = lax.ppermute(first, "core", [(0, 1), (1, 0)])
    core = lax.axis_index("core")
    order = jnp.stack([visiting_order(core), visiting_order(1 - core)])
    near, far = pair_terms(order, own, first, second, kernel, right, left)
    near = scattered(near.reshape(-1, LANES)).reshape(2, NEAR, PACKED, LANES)
    far = scattered(far.reshape(-1, 8 * LANES)).reshape(2, FAR, PACKED, LANES)
    total = jnp.concatenate([both_places(near), both_places(far)])
    return unpack(total).reshape(orbitals.shape)


def solution(mesh):
    fine = Mesh(mesh.devices.reshape(SIZES), AXES)
    placed = P(BAND, GRID, None)
    return jax.shard_map(
        body, mesh=fine, in_specs=(placed,), out_specs=placed, check_vma=False
    )
```

```python
import functools
import math

import jax
import jax.numpy as jnp
import numpy as np
from jax import lax
from jax.experimental import pallas as pl
from jax.experimental.pallas import tpu as pltpu
from jax.sharding import Mesh
from jax.sharding import PartitionSpec as P

MIXING = 0.25
SPACING = 0.31
SCREENING = 0.106

NG = 96
LANES = 128
SLAB = 6
BF16 = jnp.bfloat16
F32 = jnp.float32
AXES = ("zh", "x", "core", "y", "zl")
SIZES = (4, 4, 2, 8, 2)
BAND = ("zh", "x", "core")
GRID = ("y", "zl")
BATCH = 24
SLABS = BATCH // SLAB
VMEM_MIB = 58
NEAR = 4
FAR = SLAB - NEAR
PITCH = NG + 8
UNROLL = 1


def cas_halves():
    index = np.arange(NG)
    phases = (index[:, None] * index[None, :] % NG) * (2.0 * math.pi / NG)
    table = np.cos(phases) + np.sin(phases)
    high = table.astype(BF16)
    low = (table - high.astype(np.float64)).astype(BF16)
    return high, low


def right_table():
    high, low = cas_halves()
    table = np.zeros((2 * LANES, 2 * LANES), BF16)
    for row in (0, LANES):
        table[row : row + NG, 0:NG] = high
        table[row : row + NG, LANES : LANES + NG] = low
    return table


def left_table():
    high, low = cas_halves()
    return np.concatenate(
        [np.concatenate([high, high], axis=1), np.concatenate([low, low], axis=1)], axis=0
    )


def kernel_table(index):
    signed = jnp.where(index * 2 < NG, index, index - NG).astype(F32)
    wave = signed * (2.0 * math.pi / (NG * SPACING))
    wave_z = jnp.pad(wave, (0, LANES - NG))
    square = (
        (wave * wave)[: NG // 2 + 1, None, None] + (wave * wave)[None, :, None] + (wave_z * wave_z)[None, None, :]
    )
    safe = jnp.where(square > 0, square, 1.0)
    values = 4.0 * math.pi * (1.0 - jnp.exp(-safe / (4.0 * SCREENING * SCREENING))) / safe
    return jnp.where(square > 0, values, 0.0) * (-MIXING / float(NG) ** 3)


def halves(values):
    high = values.astype(BF16)
    low = (values - high.astype(F32)).astype(BF16)
    return high, low


def left_transform(table, columns):
    high, low = halves(columns)
    both = jnp.dot(table, jnp.concatenate([high, low], axis=0), preferred_element_type=F32)
    return both[:NG] + both[NG:]


def right_transform(rows, table):
    high, low = halves(rows)
    both = jnp.dot(jnp.concatenate([high, low], axis=1), table, preferred_element_type=F32)
    return both[:, :LANES] + both[:, LANES:]


PACKED = NG * NG // LANES
TAIL = NG - PACKED
REST = LANES - NG


def pack(planes):
    tail = planes[:, PACKED:]
    thirds = [tail[:, :, REST * at : REST * (at + 1)] for at in range(NG // REST)]
    return jnp.concatenate([planes[:, :PACKED], jnp.concatenate(thirds, axis=1)], axis=2)


def unpack(packed):
    side = packed[:, :, NG:]
    thirds = [side[:, TAIL * at : TAIL * (at + 1)] for at in range(NG // REST)]
    return jnp.concatenate([packed[:, :, :NG], jnp.concatenate(thirds, axis=2)], axis=1)


def lane_mask(rows, low, high):
    lane = lax.broadcasted_iota(jnp.int32, (rows, LANES), 1)
    return (lane >= low) & (lane < high)


def unpack_plane(packed):
    top = jnp.where(lane_mask(PACKED, 0, NG), packed, 0.0)
    tail = jnp.zeros((TAIL, LANES), packed.dtype)
    for at in range(NG // REST):
        rolled = pltpu.roll(packed[TAIL * at : TAIL * (at + 1)], REST * (at + 1), 1)
        tail = jnp.where(lane_mask(TAIL, REST * at, REST * (at + 1)), rolled, tail)
    return jnp.concatenate([top, tail], axis=0)


def pack_plane(plane):
    tail = plane[PACKED:]
    sides = [pltpu.roll(tail, LANES - REST * (at + 1), 1) for at in range(NG // REST)]
    return jnp.where(lane_mask(PACKED, 0, NG), plane[:PACKED], jnp.concatenate(sides, axis=0))


def place(pair, plane):
    return pl.ds(pl.multiple_of((pair * NG + plane) * PITCH, 8), NG)


def line(pair, ky):
    return pl.ds(pair * NG * PITCH + ky, NG, stride=PITCH)


def side_by_side(tiles):
    return jnp.concatenate(tiles, axis=1)


def stacked(tiles):
    return jnp.concatenate(tiles, axis=0)


def lane_tiles(wide):
    return [wide[:, at : at + LANES] for at in range(0, wide.shape[1], LANES)]


def row_tiles(tall):
    return [tall[at : at + NG] for at in range(0, tall.shape[0], NG)]


def pairs_kernel(order_ref, own_ref, *refs):
    *visitor_refs, right_ref, left_ref, kernel_ref, near_ref, far_ref, field, weights, arrived = refs
    weights_copy = pltpu.make_async_copy(kernel_ref, weights, arrived)
    step = pl.program_id(0)
    steps = NG // BATCH
    right = right_ref[...]
    left = left_ref[...]

    def visitor(pair, plane):
        slab = lax.rem(plane // SLAB + order_ref[pair, steps], SLABS)
        return visitor_refs[pair][slab * SLAB + plane % SLAB].astype(F32)

    @pl.when(step == 0)
    def fetch():
        weights_copy.start()

    @pl.when(step == steps)
    def fetched():
        weights_copy.wait()

    @pl.when(step < steps)
    def forward():
        rows = []
        for at in range(BATCH):
            own = own_ref[at].astype(F32)
            rows += [unpack_plane(own * visitor(pair, at)) for pair in range(2)]
        rows = right_transform(stacked(rows), right)
        columns = left_transform(left, side_by_side(row_tiles(rows)))
        for at, tile in enumerate(lane_tiles(columns)):
            field[place(at % 2, step * BATCH + at // 2), :] = tile

    @pl.when((step >= steps) & (step < 2 * steps))
    def middle():
        first = (step - steps) * BATCH
        lines = [line(at % 2, first + at // 2) for at in range(2 * BATCH)]
        columns = left_transform(left, side_by_side([field[at, :] for at in lines]))
        rows = [jnp.minimum(first + at, NG - first - at) for at in range(BATCH)]
        columns = columns * side_by_side([weights[rows[at // 2]] for at in range(2 * BATCH)])
        columns = left_transform(left, columns)
        for at, tile in zip(lines, lane_tiles(columns), strict=True):
            field[at, :] = tile

    @pl.when(step >= 2 * steps)
    def backward():
        first = (step - 2 * steps) * BATCH
        tiles = [field[place(at % 2, first + at // 2), :] for at in range(2 * BATCH)]
        columns = left_transform(left, side_by_side(tiles))
        tiles = row_tiles(right_transform(stacked(lane_tiles(columns)), right))
        for at in range(BATCH):
            terms = [pack_plane(tiles[2 * at + pair]) * visitor(pair, at) for pair in range(2)]
            slab, plane = divmod(at, SLAB)
            if plane < NEAR:
                near_ref[slab * NEAR + plane] = terms[0] + terms[1]
            else:
                far_ref[slab * FAR + plane - NEAR] = terms[0] + terms[1]


CUBE = (NG, PACKED, LANES)


def pair_terms(order, own, first, second, kernel, right, left):
    steps = NG // BATCH

    def clipped(i, low):
        return jnp.clip(i - low, 0, steps - 1)

    def both(i):
        return jnp.where(i < steps, i, clipped(i, 2 * steps))

    def planes(count, place_of):
        return pl.BlockSpec((count, PACKED, LANES), lambda i, order: (place_of(i, order), 0, 0))

    def visitor(pair):
        return planes(BATCH, lambda i, order: order[pair, both(i)])

    return pl.pallas_call(
        pairs_kernel,
        grid_spec=pltpu.PrefetchScalarGridSpec(
            num_scalar_prefetch=1,
            grid=(3 * steps,),
            in_specs=[
                planes(BATCH, lambda i, order: clipped(i, 0)),
                visitor(0),
                visitor(1),
                pl.BlockSpec((2 * LANES, 2 * LANES), lambda i, order: (0, 0)),
                pl.BlockSpec((2 * NG, 2 * NG), lambda i, order: (0, 0)),
                pl.BlockSpec(memory_space=pl.ANY),
            ],
            out_specs=[
                planes(count * SLABS, lambda i, order: clipped(i, 2 * steps)) for count in (NEAR, FAR)
            ],
            scratch_shapes=[
                pltpu.VMEM((2 * NG * PITCH, LANES), F32),
                pltpu.VMEM((NG // 2 + 1, NG, LANES), F32),
                pltpu.SemaphoreType.DMA,
            ],
        ),
        out_shape=[
            jax.ShapeDtypeStruct((NG // SLAB * count, PACKED, LANES), F32) for count in (NEAR, FAR)
        ],
        compiler_params=pltpu.CompilerParams(vmem_limit_bytes=VMEM_MIB * 1024 * 1024),
        cost_estimate=pl.CostEstimate(
            flops=4 * 6 * NG * NG * 256 * 256, bytes_accessed=17_000_000, transcendentals=0
        ),
        name="pair_terms",
    )(order, own, first, second, right, left, kernel)


def meeting_place(zh, x, core):
    return (zh + 4 * ((x % 2 + core) % 2)) % 8, x // 2


def landing(zh, x, y, zl, meeting_y):
    apart = (y - meeting_y // 2 * 2) % 8
    return (zh + 2 * (apart % 2) + zl) % 4, (x + apart // 2) % 4


def exchanged_slabs(slab):
    pairs = []
    for zh, x, core, y, zl in np.ndindex(*SIZES):
        there_y, there_zl = meeting_place(zh, x, core)
        there_zh, there_x = landing(zh, x, y, zl, there_y)
        target = (there_zh, there_x, core, there_y, there_zl)
        pairs.append(
            (int(np.ravel_multi_index((zh, x, core, y, zl), SIZES)), int(np.ravel_multi_index(target, SIZES)))
        )
    return lax.ppermute(slab, AXES, pairs)


def visiting_order(core):
    y, zl = lax.axis_index("y"), lax.axis_index("zl")
    zh = y % 4
    x = 2 * zl + (y // 4 + core) % 2
    block = jnp.arange(4, dtype=jnp.int32)
    apart = (x + block - y // 2 - lax.axis_index("x")) % 4
    place = jnp.where(apart == 3, 1, jnp.where(apart == 0, 0, apart + 1))
    return jnp.concatenate([place, zh[None]]).astype(jnp.int32)


def gathered_x(block):
    def shifted(part, by):
        return lax.ppermute(part, "x", [(at, (at + by) % 4) for at in range(4)])

    before, after = shifted(block, 1), shifted(block, 3)
    return [block, before, after, shifted(before[:2], 1), shifted(after[2:], 3)]


def gathered(block, axis):
    return lax.all_gather(block, axis, axis=0, tiled=True)


def scattered(terms):
    return lax.psum_scatter(terms, "y", scatter_dimension=0, tiled=True)


def both_places(slabs):
    place = lax.axis_index("zl")
    mine = lax.dynamic_index_in_dim(slabs, place, keepdims=False)
    other = lax.dynamic_index_in_dim(slabs, 1 - place, keepdims=False)
    return mine + lax.ppermute(other, "zl", [(0, 1), (1, 0)])


def body(orbitals):
    slab = pack(orbitals.reshape(SLAB, NG, NG)).reshape(SLAB * PACKED, LANES)
    right = jnp.asarray(right_table())
    left = jnp.asarray(left_table())
    visiting = exchanged_slabs(slab)
    pair = gathered(slab, "zl")
    pair, visiting = lax.optimization_barrier((pair, visiting))
    own = gathered(pair, "y").reshape(CUBE)
    blocks = gathered_x(gathered(visiting[None], "zh"))
    index = jnp.arange(NG, dtype=jnp.int32)
    own, index = lax.optimization_barrier((own, index))
    kernel = kernel_table(index)
    first = jnp.concatenate(blocks).reshape(CUBE)
    second = lax.ppermute(first, "core", [(0, 1), (1, 0)])
    core = lax.axis_index("core")
    order = jnp.stack([visiting_order(core), visiting_order(1 - core)])
    near, far = pair_terms(order, own, first, second, kernel, right, left)
    near = scattered(near.reshape(-1, LANES)).reshape(2, NEAR, PACKED, LANES)
    far = scattered(far.reshape(-1, 8 * LANES)).reshape(2, FAR, PACKED, LANES)
    total = jnp.concatenate([both_places(near), both_places(far)])
    return unpack(total).reshape(orbitals.shape)


def solution(mesh):
    fine = Mesh(mesh.devices.reshape(SIZES), AXES)
    placed = P(BAND, GRID, None)
    return jax.shard_map(
        body, mesh=fine, in_specs=(placed,), out_specs=placed, check_vma=False
    )
```

```python
import functools
import math

import jax
import jax.numpy as jnp
import numpy as np
from jax import lax
from jax.experimental import pallas as pl
from jax.experimental.pallas import tpu as pltpu
from jax.sharding import Mesh
from jax.sharding import PartitionSpec as P

MIXING = 0.25
SPACING = 0.31
SCREENING = 0.106

NG = 96
LANES = 128
SLAB = 6
BF16 = jnp.bfloat16
F32 = jnp.float32
AXES = ("zh", "x", "core", "y", "zl")
SIZES = (4, 4, 2, 8, 2)
BAND = ("zh", "x", "core")
GRID = ("y", "zl")
BATCH = 24
SLABS = BATCH // SLAB
VMEM_MIB = 58
NEAR = 4
FAR = SLAB - NEAR
PITCH = NG + 8
UNROLL = 1


def cas_halves():
    index = np.arange(NG)
    phases = (index[:, None] * index[None, :] % NG) * (2.0 * math.pi / NG)
    table = np.cos(phases) + np.sin(phases)
    high = table.astype(BF16)
    low = (table - high.astype(np.float64)).astype(BF16)
    return high, low


def right_table():
    high, low = cas_halves()
    table = np.zeros((2 * LANES, 2 * LANES), BF16)
    for row in (0, LANES):
        table[row : row + NG, 0:NG] = high
        table[row : row + NG, LANES : LANES + NG] = low
    return table


def left_table():
    high, low = cas_halves()
    return np.concatenate(
        [np.concatenate([high, high], axis=1), np.concatenate([low, low], axis=1)], axis=0
    )


def kernel_table(index):
    signed = jnp.where(index * 2 < NG, index, index - NG).astype(F32)
    wave = signed * (2.0 * math.pi / (NG * SPACING))
    wave_z = jnp.pad(wave, (0, LANES - NG))
    square = (
        (wave * wave)[: NG // 2 + 1, None, None] + (wave * wave)[None, :, None] + (wave_z * wave_z)[None, None, :]
    )
    safe = jnp.where(square > 0, square, 1.0)
    values = 4.0 * math.pi * (1.0 - jnp.exp(-safe / (4.0 * SCREENING * SCREENING))) / safe
    return jnp.where(square > 0, values, 0.0) * (-MIXING / float(NG) ** 3)


def halves(values):
    high = values.astype(BF16)
    low = (values - high.astype(F32)).astype(BF16)
    return high, low


def left_transform(table, columns):
    high, low = halves(columns)
    both = jnp.dot(table, jnp.concatenate([high, low], axis=0), preferred_element_type=F32)
    return both[:NG] + both[NG:]


def right_transform(rows, table):
    high, low = halves(rows)
    both = jnp.dot(jnp.concatenate([high, low], axis=1), table, preferred_element_type=F32)
    return both[:, :LANES] + both[:, LANES:]


PACKED = NG * NG // LANES
TAIL = NG - PACKED
REST = LANES - NG


def pack(planes):
    tail = planes[:, PACKED:]
    thirds = [tail[:, :, REST * at : REST * (at + 1)] for at in range(NG // REST)]
    return jnp.concatenate([planes[:, :PACKED], jnp.concatenate(thirds, axis=1)], axis=2)


def unpack(packed):
    side = packed[:, :, NG:]
    thirds = [side[:, TAIL * at : TAIL * (at + 1)] for at in range(NG // REST)]
    return jnp.concatenate([packed[:, :, :NG], jnp.concatenate(thirds, axis=2)], axis=1)


def lane_mask(rows, low, high):
    lane = lax.broadcasted_iota(jnp.int32, (rows, LANES), 1)
    return (lane >= low) & (lane < high)


def unpack_plane(packed):
    top = jnp.where(lane_mask(PACKED, 0, NG), packed, 0.0)
    tail = jnp.zeros((TAIL, LANES), packed.dtype)
    for at in range(NG // REST):
        rolled = pltpu.roll(packed[TAIL * at : TAIL * (at + 1)], REST * (at + 1), 1)
        tail = jnp.where(lane_mask(TAIL, REST * at, REST * (at + 1)), rolled, tail)
    return jnp.concatenate([top, tail], axis=0)


def pack_plane(plane):
    tail = plane[PACKED:]
    sides = [pltpu.roll(tail, LANES - REST * (at + 1), 1) for at in range(NG // REST)]
    return jnp.where(lane_mask(PACKED, 0, NG), plane[:PACKED], jnp.concatenate(sides, axis=0))


def place(pair, plane):
    return pl.ds(pl.multiple_of((pair * NG + plane) * PITCH, 8), NG)


def line(pair, ky):
    return pl.ds(pair * NG * PITCH + ky, NG, stride=PITCH)


def side_by_side(tiles):
    return jnp.concatenate(tiles, axis=1)


def stacked(tiles):
    return jnp.concatenate(tiles, axis=0)


def lane_tiles(wide):
    return [wide[:, at : at + LANES] for at in range(0, wide.shape[1], LANES)]


def row_tiles(tall):
    return [tall[at : at + NG] for at in range(0, tall.shape[0], NG)]


def pairs_kernel(order_ref, own_ref, *refs):
    *visitor_refs, right_ref, left_ref, kernel_ref, near_ref, far_ref, field, weights, arrived = refs
    weights_copy = pltpu.make_async_copy(kernel_ref, weights, arrived)
    step = pl.program_id(0)
    steps = NG // BATCH
    right = right_ref[...]
    left = left_ref[...]

    def visitor(pair, plane):
        slab = lax.rem(plane // SLAB + order_ref[pair, steps], SLABS)
        return visitor_refs[pair][slab * SLAB + plane % SLAB].astype(F32)

    @pl.when(step == 0)
    def fetch():
        weights_copy.start()

    @pl.when(step == steps)
    def fetched():
        weights_copy.wait()

    @pl.when(step < steps)
    def forward():
        rows = []
        for at in range(BATCH):
            own = own_ref[at].astype(F32)
            rows += [unpack_plane(own * visitor(pair, at)) for pair in range(2)]
        rows = right_transform(stacked(rows), right)
        columns = left_transform(left, side_by_side(row_tiles(rows)))
        for at, tile in enumerate(lane_tiles(columns)):
            field[place(at % 2, step * BATCH + at // 2), :] = tile

    @pl.when((step >= steps) & (step < 2 * steps))
    def middle():
        first = (step - steps) * BATCH
        lines = [line(at % 2, first + at // 2) for at in range(2 * BATCH)]
        columns = left_transform(left, side_by_side([field[at, :] for at in lines]))
        rows = [jnp.minimum(first + at, NG - first - at) for at in range(BATCH)]
        columns = columns * side_by_side([weights[rows[at // 2]] for at in range(2 * BATCH)])
        columns = left_transform(left, columns)
        for at, tile in zip(lines, lane_tiles(columns), strict=True):
            field[at, :] = tile

    @pl.when(step >= 2 * steps)
    def backward():
        first = (step - 2 * steps) * BATCH
        tiles = [field[place(at % 2, first + at // 2), :] for at in range(2 * BATCH)]
        columns = left_transform(left, side_by_side(tiles))
        tiles = row_tiles(right_transform(stacked(lane_tiles(columns)), right))
        for at in range(BATCH):
            terms = [pack_plane(tiles[2 * at + pair]) * visitor(pair, at) for pair in range(2)]
            slab, plane = divmod(at, SLAB)
            if plane < NEAR:
                near_ref[slab * NEAR + plane] = terms[0] + terms[1]
            else:
                far_ref[slab * FAR + plane - NEAR] = terms[0] + terms[1]


CUBE = (NG, PACKED, LANES)


def pair_terms(order, own, first, second, kernel, right, left):
    steps = NG // BATCH

    def clipped(i, low):
        return jnp.clip(i - low, 0, steps - 1)

    def both(i):
        return jnp.where(i < steps, i, clipped(i, 2 * steps))

    def planes(count, place_of):
        return pl.BlockSpec((count, PACKED, LANES), lambda i, order: (place_of(i, order), 0, 0))

    def visitor(pair):
        return planes(BATCH, lambda i, order: order[pair, both(i)])

    return pl.pallas_call(
        pairs_kernel,
        grid_spec=pltpu.PrefetchScalarGridSpec(
            num_scalar_prefetch=1,
            grid=(3 * steps,),
            in_specs=[
                planes(BATCH, lambda i, order: clipped(i, 0)),
                visitor(0),
                visitor(1),
                pl.BlockSpec((2 * LANES, 2 * LANES), lambda i, order: (0, 0)),
                pl.BlockSpec((2 * NG, 2 * NG), lambda i, order: (0, 0)),
                pl.BlockSpec(memory_space=pl.ANY),
            ],
            out_specs=[
                planes(count * SLABS, lambda i, order: clipped(i, 2 * steps)) for count in (NEAR, FAR)
            ],
            scratch_shapes=[
                pltpu.VMEM((2 * NG * PITCH + PITCH, LANES), F32),
                pltpu.VMEM((NG // 2 + 1, NG, LANES), F32),
                pltpu.SemaphoreType.DMA,
            ],
        ),
        out_shape=[
            jax.ShapeDtypeStruct((NG // SLAB * count, PACKED, LANES), F32) for count in (NEAR, FAR)
        ],
        compiler_params=pltpu.CompilerParams(vmem_limit_bytes=VMEM_MIB * 1024 * 1024),
        cost_estimate=pl.CostEstimate(
            flops=4 * 6 * NG * NG * 256 * 256, bytes_accessed=17_000_000, transcendentals=0
        ),
        name="pair_terms",
    )(order, own, first, second, right, left, kernel)


def meeting_place(zh, x, core):
    return (zh + 4 * ((x % 2 + core) % 2)) % 8, x // 2


def landing(zh, x, y, zl, meeting_y):
    apart = (y - meeting_y // 2 * 2) % 8
    return (zh + 2 * (apart % 2) + zl) % 4, (x + apart // 2) % 4


def exchanged_slabs(slab):
    pairs = []
    for zh, x, core, y, zl in np.ndindex(*SIZES):
        there_y, there_zl = meeting_place(zh, x, core)
        there_zh, there_x = landing(zh, x, y, zl, there_y)
        target = (there_zh, there_x, core, there_y, there_zl)
        pairs.append(
            (int(np.ravel_multi_index((zh, x, core, y, zl), SIZES)), int(np.ravel_multi_index(target, SIZES)))
        )
    return lax.ppermute(slab, AXES, pairs)


def visiting_order(core):
    y, zl = lax.axis_index("y"), lax.axis_index("zl")
    zh = y % 4
    x = 2 * zl + (y // 4 + core) % 2
    block = jnp.arange(4, dtype=jnp.int32)
    apart = (x + block - y // 2 - lax.axis_index("x")) % 4
    place = jnp.where(apart == 3, 1, jnp.where(apart == 0, 0, apart + 1))
    return jnp.concatenate([place, zh[None]]).astype(jnp.int32)


def gathered_x(block):
    def shifted(part, by):
        return lax.ppermute(part, "x", [(at, (at + by) % 4) for at in range(4)])

    before, after = shifted(block, 1), shifted(block, 3)
    return [block, before, after, shifted(before[:2], 1), shifted(after[2:], 3)]


def gathered(block, axis):
    return lax.all_gather(block, axis, axis=0, tiled=True)


def scattered(terms):
    return lax.psum_scatter(terms, "y", scatter_dimension=0, tiled=True)


def both_places(slabs):
    place = lax.axis_index("zl")
    mine = lax.dynamic_index_in_dim(slabs, place, keepdims=False)
    other = lax.dynamic_index_in_dim(slabs, 1 - place, keepdims=False)
    return mine + lax.ppermute(other, "zl", [(0, 1), (1, 0)])


def body(orbitals):
    slab = pack(orbitals.reshape(SLAB, NG, NG)).reshape(SLAB * PACKED, LANES)
    right = jnp.asarray(right_table())
    left = jnp.asarray(left_table())
    visiting = exchanged_slabs(slab)
    pair = gathered(slab, "zl")
    pair, visiting = lax.optimization_barrier((pair, visiting))
    own = gathered(pair, "y").reshape(CUBE)
    blocks = gathered_x(gathered(visiting[None], "zh"))
    index = jnp.arange(NG, dtype=jnp.int32)
    own, index = lax.optimization_barrier((own, index))
    kernel = kernel_table(index)
    first = jnp.concatenate(blocks).reshape(CUBE)
    second = lax.ppermute(first, "core", [(0, 1), (1, 0)])
    core = lax.axis_index("core")
    order = jnp.stack([visiting_order(core), visiting_order(1 - core)])
    near, far = pair_terms(order, own, first, second, kernel, right, left)
    near = scattered(near.reshape(-1, LANES)).reshape(2, NEAR, PACKED, LANES)
    far = scattered(far.reshape(-1, 8 * LANES)).reshape(2, FAR, PACKED, LANES)
    total = jnp.concatenate([both_places(near), both_places(far)])
    return unpack(total).reshape(orbitals.shape)


def solution(mesh):
    fine = Mesh(mesh.devices.reshape(SIZES), AXES)
    placed = P(BAND, GRID, None)
    return jax.shard_map(
        body, mesh=fine, in_specs=(placed,), out_specs=placed, check_vma=False
    )
```
